32 devices in a mesh: shift: 4 (over y, core), space: 8 (over z, x).
Axes of the slice: x: 2, y: 2, z: 4, core: 2. Of those that a mesh axis runs over, the one named last changes fastest.
Arguments:
- coefficients: float32 [4, 2, 2, 8, 32, 512], P('shift', None, None, 'space'), may hold values from -0.18 to 0.18
- source: float32 [8, 8, 8, 256], P('space'), may hold values from -26 to 26
Outputs:
- pressure_mean: float32 [8, 8, 8, 256], P('space')
- pressure_variance: float32 [8, 8, 8, 256], P('space')
The draws below stay inside these ranges and needn't reach their ends.
All inputs are finite; a program needn't handle non-finite values.
Results may differ from the reference program's by a relative error of at most 0.0004.
Values sent between devices are 32-bit elements; how exact they have to be, the bound alone decides.
A program may use at most 64 MiB of HBM per device.

```python
import jax
import jax.numpy as jnp
from jax import lax

YB = 8
NZE = 512
ITERS = 4
BX = 2
BY = 4
BRICKS = 8
XB = 8
NX = 16
NY = 32
NZ = 256
SHIFTS = 4


def draw_source(key, part):
    key = jax.random.fold_in(key, 7)
    key_normal = jax.random.fold_in(key, 0)
    roughness = 4.0 * jnp.clip(jax.random.normal(key_normal, (BRICKS, XB, YB, NZ), jnp.float32), -4.0, 4.0)
    return roughness


def steps_of(key, shape, shards, smallest, largest):
    loudness, own = 1.0, jax.random.fold_in(key, 6)
    for dim, shards_of in shards:
        steps = jnp.exp(jax.random.uniform(jax.random.fold_in(own, dim), (shards_of,), jnp.float32, smallest / len(shards), largest / len(shards)))
        loudness = loudness * jnp.repeat(steps, shape[dim] // shards_of).reshape([-1 if axis == dim else 1 for axis in range(len(shape))])
    return loudness


def bell_draw(key, shape, width, bound, cuts=(), held_as=jnp.bfloat16):
    gain = steps_of(key, shape, cuts, -0.22, 0.18) if cuts else 1.0
    entries = jax.random.normal(key, shape, jnp.float32) * width * gain
    return jnp.minimum(jnp.maximum(entries, -bound), bound).astype(held_as)


def setup_inputs(seed: int = 0) -> dict:
    seeds = jax.random.split(jax.random.key(seed), 3)
    coefficients = bell_draw(seeds[0], (SHIFTS, 2, BX, XB, NY, NZE), 0.03, 0.18, ((0, 4), (3, 8)), jnp.float32)
    source = draw_source(jax.random.fold_in(seeds[2], 71), 0)
    return dict(coefficients=coefficients, source=source)


reaction = 0.02
low_bound = 0.05
high_bound = 2.0
centre = 0.5 * (low_bound + high_bound)
half_width = 0.5 * (high_bound - low_bound)
sigma_one = centre / half_width


def harmonic(left, right):
    return 2.0 * left * right / (left + right)


def neighbours(pressure_field, which_axis):
    widths = [(1, 1) if which == which_axis else (0, 0) for which in range(3)]
    padded = jnp.pad(pressure_field, widths)
    extent = pressure_field.shape[which_axis]
    lower = lax.slice_in_dim(padded, 0, extent, axis=which_axis)
    upper = lax.slice_in_dim(padded, 2, extent + 2, axis=which_axis)
    return lower, upper


def operate(pressure_field, weight_list):
    total = reaction * pressure_field
    for which_axis in range(3):
        lower, upper = neighbours(pressure_field, which_axis)
        weight_lower, weight_upper = weight_list[which_axis]
        total = total + weight_upper * (pressure_field - upper) + weight_lower * (pressure_field - lower)
    return total


def chebyshev(perm, grid_source):
    weight_list = []
    diagonal = reaction + jnp.zeros_like(perm)
    for which_axis in range(3):
        lower, upper = neighbours(perm, which_axis)
        weight_lower = harmonic(perm, lower)
        weight_upper = harmonic(perm, upper)
        weight_list.append((weight_lower, weight_upper))
        diagonal = diagonal + (weight_lower + weight_upper)
    pressure = jnp.zeros_like(perm)
    residual = grid_source
    direction = residual / diagonal / centre
    ratio_now = 1.0 / sigma_one
    for sweep_index in range(ITERS):
        pressure = pressure + direction
        residual = residual - operate(direction, weight_list)
        ratio_next = 1.0 / (2.0 * sigma_one - ratio_now)
        direction = ratio_next * ratio_now * direction + (2.0 * ratio_next / half_width) * (residual / diagonal)
        ratio_now = ratio_next
    return pressure + direction


def unbrick(bricks):
    shaped = bricks.reshape(BX, BY, XB, YB, NZ)
    return shaped.transpose(0, 2, 1, 3, 4).reshape(NX, NY, NZ)


def brick(pressure_field):
    shaped = pressure_field.reshape(BX, XB, BY, YB, NZ)
    return shaped.transpose(0, 2, 1, 3, 4).reshape(BRICKS, XB, YB, NZ)


def reference(coefficients, source):
    grid_source = unbrick(source)

    def solve_shift(spectral):
        spectrum = lax.complex(spectral[0], spectral[1]).reshape(NX, NY, NZE)
        logperm = jnp.real(jnp.fft.fft(spectrum, axis=-1))[:, :, :NZ]
        perm = jnp.exp(logperm)
        return chebyshev(perm, grid_source)

    pressures = lax.map(solve_shift, coefficients)
    first = jnp.sum(pressures, axis=0)
    second = jnp.sum(pressures * pressures, axis=0)
    count = coefficients.shape[0]
    pressure_mean = first / count
    pressure_variance = (second - first * pressure_mean) / (count - 1)
    return brick(pressure_mean), brick(pressure_variance)
```

```python
import functools
import math

import jax
import jax.numpy as jnp
import ml_dtypes
import numpy as np
from jax import lax
from jax.experimental import pallas as pl
from jax.experimental.pallas import tpu as pltpu
from jax.sharding import PartitionSpec as P

ITERS = 4
MESH = pl.DeviceIdType.MESH
SLABS = 8
SLAB = 32
MARGIN = 16
QUARTERS = 4


reaction = 0.02
low_bound = 0.05
high_bound = 2.0
centre = 0.5 * (low_bound + high_bound)
half_width = 0.5 * (high_bound - low_bound)
sigma_one = centre / half_width


def passed_along(value, axis, steps):
    count = lax.axis_size(axis)
    first, last = (max(0, -steps), min(count, count - steps))
    return lax.ppermute(value, axis, [(source, source + steps) for source in range(first, last)])


def harmonic(left, right):
    return 2.0 * left * right / (left + right)


def carry_first(layer, offset):
    return passed_along(layer, "space", offset)


def carry_second(layer, offset):
    return passed_along(layer, "space", offset)


def lower_and_upper(
    pressure_field, which_axis, index_step, axis_position, bricks_along, halo_holder
):
    extent = pressure_field.shape[which_axis]
    highest_layer = lax.slice_in_dim(pressure_field, extent - 1, extent, axis=which_axis)
    lowest_layer = lax.slice_in_dim(pressure_field, 0, 1, axis=which_axis)
    lower_mask = (axis_position > 0).astype(jnp.float32)
    upper_mask = (axis_position < bricks_along - 1).astype(jnp.float32)
    received_below = halo_holder(highest_layer, index_step) * lower_mask
    received_above = halo_holder(lowest_layer, -index_step) * upper_mask
    lower = jnp.concatenate(
        [received_below, lax.slice_in_dim(pressure_field, 0, extent - 1, axis=which_axis)],
        axis=which_axis,
    )
    upper = jnp.concatenate(
        [lax.slice_in_dim(pressure_field, 1, extent, axis=which_axis), received_above],
        axis=which_axis,
    )
    return (lower, upper)


def along_depth(pressure_field, which_axis):
    extent = pressure_field.shape[which_axis]
    blank = jnp.zeros_like(lax.slice_in_dim(pressure_field, 0, 1, axis=which_axis))
    lower = jnp.concatenate(
        [blank, lax.slice_in_dim(pressure_field, 0, extent - 1, axis=which_axis)], axis=which_axis
    )
    upper = jnp.concatenate(
        [lax.slice_in_dim(pressure_field, 1, extent, axis=which_axis), blank], axis=which_axis
    )
    return (lower, upper)


def operate(pressure_field, weight_list, finders):
    total = reaction * pressure_field
    for which_axis in range(3):
        lower, upper = finders[which_axis](pressure_field)
        weight_lower, weight_upper = weight_list[which_axis]
        total = (
            total
            + weight_upper * (pressure_field - upper)
            + weight_lower * (pressure_field - lower)
        )
    return total


def shards(coefficients, source):
    n_space = lax.axis_size("space")
    bricks_first = max(2, n_space // 8)
    bricks_second = n_space // bricks_first
    position = lax.axis_index("space")
    brick_x = position // bricks_second
    brick_y = position % bricks_second
    local = coefficients[0]
    modes_count = local.shape[-1]
    columns = local.shape[3]
    cells_z = modes_count // 2
    pencils = local.reshape(2, bricks_first * columns, modes_count)
    modes = lax.broadcasted_iota(jnp.int32, (modes_count, cells_z), 0)
    cells = lax.broadcasted_iota(jnp.int32, (modes_count, cells_z), 1)
    angle = (modes * cells % modes_count).astype(jnp.float32) * (2.0 * math.pi / modes_count)
    logperm = jnp.dot(
        pencils[0],
        jnp.cos(angle),
        precision=lax.Precision.HIGHEST,
        preferred_element_type=jnp.float32,
    )
    logperm = logperm + jnp.dot(
        pencils[1],
        jnp.sin(angle),
        precision=lax.Precision.HIGHEST,
        preferred_element_type=jnp.float32,
    )
    perm_rows = jnp.exp(logperm)
    brick_cols = columns // bricks_second
    n_shift = lax.axis_size("shift")
    outgoing = perm_rows.reshape(n_space, 1, brick_cols, cells_z)
    arrived = lax.all_to_all(outgoing, "space", split_axis=0, concat_axis=1, tiled=True)
    perm = arrived.reshape(n_space, brick_cols, cells_z)

    def find_first(pressure_field):
        return lower_and_upper(pressure_field, 0, bricks_second, brick_x, bricks_first, carry_first)

    def find_second(pressure_field):
        return lower_and_upper(pressure_field, 1, 1, brick_y, bricks_second, carry_second)

    def find_third(pressure_field):
        return along_depth(pressure_field, 2)

    residual = source[0]
    finders = [find_first, find_second, find_third]
    weight_list = []
    diagonal = reaction + jnp.zeros_like(perm)
    for which_axis in range(3):
        lower, upper = finders[which_axis](perm)
        weight_lower = harmonic(perm, lower)
        weight_upper = harmonic(perm, upper)
        weight_list.append((weight_lower, weight_upper))
        diagonal = diagonal + (weight_lower + weight_upper)
    pressure = jnp.zeros_like(perm)
    direction = residual / diagonal / centre
    ratio_now = 1.0 / sigma_one
    for sweep_index in range(ITERS):
        pressure = pressure + direction
        residual = residual - operate(direction, weight_list, finders)
        ratio_next = 1.0 / (2.0 * sigma_one - ratio_now)
        direction = ratio_next * ratio_now * direction + 2.0 * ratio_next / half_width * (
            residual / diagonal
        )
        ratio_now = ratio_next
    pressure = pressure + direction
    first, second = lax.psum((pressure, pressure * pressure), "shift")
    pressure_mean = first / n_shift
    pressure_variance = (second - first * pressure_mean) / (n_shift - 1)
    return (pressure_mean[None], pressure_variance[None])


def lanes_of(value):
    return lax.broadcasted_iota(jnp.int32, value.shape, value.ndim - 1)


def roll_lanes(value, shift):
    shift = shift % value.shape[-1]
    return pltpu.roll(value, shift, value.ndim - 1) if shift else value


def window(low, high, slab, offset):
    start = (SLAB * slab - MARGIN) % 128
    shift = 128 - start + offset
    begin = SLAB * slab - MARGIN
    if begin + 64 <= 128 or slab == 0:
        return roll_lanes(low, shift)
    if begin >= 128:
        return roll_lanes(high, shift)
    return jnp.where(
        lanes_of(low) < 128 - start + offset, roll_lanes(low, shift), roll_lanes(high, shift)
    )


def window_pair(first, second, slab):
    left = window(first[..., :128], first[..., 128:], slab, 0)
    right = window(second[..., :128], second[..., 128:], slab, 64)
    return jnp.where(lanes_of(left) < 64, left, right)


def slab_kernel(
    coef_ref, source_ref, table_hbm,
    mean_ref, var_ref,
    table, src_send, src_recv, perm_send, perm_recv, w_x, w_y, w_z, rdiag, resid, direc, press,
    part_send, part_recv, brick_send, brick_recv,
    table_sem, src_ss, src_rs, perm_ss, perm_rs, part_ss, part_rs, brick_ss, brick_rs,
):
    shift = lax.axis_index("shift")
    me = lax.axis_index("space")
    by = lax.rem(me, QUARTERS)
    own = by == shift

    table_copy = pltpu.make_async_copy(table_hbm, table, table_sem)
    table_copy.start()

    barrier = pltpu.get_barrier_semaphore()
    for step in range(1, SLABS):
        pl.semaphore_signal(
            barrier, inc=1, device_id={"space": lax.rem(me + step, SLABS)}, device_id_type=MESH
        )
    for step in range(1, QUARTERS):
        pl.semaphore_signal(
            barrier, inc=1, device_id={"shift": lax.rem(shift + step, QUARTERS)}, device_id_type=MESH
        )
    for slab in range(SLABS):

        @pl.when(jnp.logical_not(jnp.logical_and(own, me == slab)))
        def _():
            pl.semaphore_signal(
                barrier, inc=1, device_id={"shift": by, "space": slab}, device_id_type=MESH
            )

    for slab in range(SLABS):
        for row in range(4):
            src_send[slab, row] = window_pair(source_ref[row], source_ref[row + 4], slab)

    pl.semaphore_wait(barrier, SLABS - 1 + QUARTERS - 1 + SLABS - own.astype(jnp.int32))

    def space_copy(send, recv, ss, rs, slot, target):
        return pltpu.make_async_remote_copy(
            src_ref=send.at[target], dst_ref=recv.at[slot], send_sem=ss.at[target],
            recv_sem=rs.at[slot], device_id={"space": target}, device_id_type=MESH,
        )

    for step in range(1, SLABS):
        space_copy(src_send, src_recv, src_ss, src_rs, me, lax.rem(me + step, SLABS)).start()
    src_recv[me] = src_send[me]

    real, imag = coef_ref[0], coef_ref[1]
    real_hi, imag_hi = real.astype(jnp.bfloat16), imag.astype(jnp.bfloat16)
    real_lo = (real - real_hi.astype(jnp.float32)).astype(jnp.bfloat16)
    imag_lo = (imag - imag_hi.astype(jnp.float32)).astype(jnp.bfloat16)
    table_copy.wait()
    dot = functools.partial(jnp.dot, preferred_element_type=jnp.float32)
    rows = real.shape[0]
    both = dot(jnp.concatenate([real_hi, real_lo], 0), table[0, 0])
    both = both + dot(jnp.concatenate([imag_hi, imag_lo], 0), table[0, 1])
    rest = dot(real_hi, table[1, 0]) + dot(imag_hi, table[1, 1])
    perm = jnp.exp(both[:rows] + (both[rows:] + rest))
    half = rows // 2
    for slab in range(SLABS):
        perm_send[slab] = window_pair(perm[:half], perm[half:], slab)
    for step in range(1, SLABS):
        space_copy(perm_send, perm_recv, perm_ss, perm_rs, me, lax.rem(me + step, SLABS)).start()
    perm_recv[me] = perm_send[me]

    for step in range(1, SLABS):
        slot = lax.rem(me + step, SLABS)
        space_copy(perm_send, perm_recv, perm_ss, perm_rs, slot, slot).wait_recv()

    shape = (32, 128)
    lane = lax.broadcasted_iota(jnp.int32, shape, 1)
    sub = lax.broadcasted_iota(jnp.int32, shape, 0)
    place = SLAB * me - MARGIN + lax.rem(lane, 64)
    inner_z = jnp.logical_and(place != -1, place != 255)
    inner_y = sub != 31
    inner_x = lane < 64

    def next_y(value):
        return pltpu.roll(value, 31, 0)

    def last_y(value):
        return pltpu.roll(value, 1, 0)

    def next_z(value):
        return roll_lanes(value, 127)

    def last_z(value):
        return roll_lanes(value, 1)

    def face_x(n):
        upper = roll_lanes(perm_recv[0], 64) if n == 7 else perm_recv[n + 1]
        weight = harmonic(perm_recv[n], upper)
        return jnp.where(inner_x, weight, 0.0) if n == 7 else weight

    last = face_x(7)
    w_x[7] = last
    lower_x = roll_lanes(last, 64)
    for n in range(8):
        cell = perm_recv[n]
        if n < 7:
            last = face_x(n)
            w_x[n] = last
        else:
            last = w_x[7]
        up_y = jnp.where(inner_y, harmonic(cell, next_y(cell)), 0.0)
        up_z = jnp.where(inner_z, harmonic(cell, next_z(cell)), 0.0)
        w_y[n] = up_y
        w_z[n] = up_z
        diagonal = reaction + (lower_x + last) + (last_y(up_y) + up_y) + (last_z(up_z) + up_z)
        rdiag[n] = 1.0 / diagonal
        lower_x = last

    for step in range(1, SLABS):
        slot = lax.rem(me + step, SLABS)
        space_copy(src_send, src_recv, src_ss, src_rs, slot, slot).wait_recv()
    left8 = lax.broadcasted_iota(jnp.int32, (8, 128), 1) < 64
    for n in range(8):
        for brick_y in range(QUARTERS):
            near, far = src_recv[brick_y, n % 4], src_recv[QUARTERS + brick_y, n % 4]
            if n < 4:
                far = roll_lanes(far, 64)
            else:
                near = roll_lanes(near, 64)
            piece = jnp.where(left8, near, far)
            rows_y = slice(brick_y * 8, brick_y * 8 + 8)
            resid[n, rows_y] = piece
            direc[n, rows_y] = piece * rdiag[n, rows_y] * (1.0 / centre)

    ratio_now = 1.0 / sigma_one
    for sweep in range(ITERS):
        ratio_next = 1.0 / (2.0 * sigma_one - ratio_now)
        keep, gain = ratio_next * ratio_now, 2.0 * ratio_next / half_width
        ratio_now = ratio_next
        first_next = roll_lanes(direc[0], 64)
        flux_last = w_x[7] * (direc[7] - first_next)
        lower_flux = roll_lanes(flux_last, 64)
        for n in range(8):
            now = direc[n]
            flux = w_x[n] * (now - direc[n + 1]) if n < 7 else flux_last
            flux_y = w_y[n] * (now - next_y(now))
            flux_z = w_z[n] * (now - next_z(now))
            total = reaction * now + (flux - lower_flux)
            total = total + (flux_y - last_y(flux_y)) + (flux_z - last_z(flux_z))
            lower_flux = flux
            left_over = resid[n] - total
            if sweep < ITERS - 1:
                resid[n] = left_over
            new = keep * now + gain * (left_over * rdiag[n])
            so_far = now + press[n] if sweep else now
            if sweep < ITERS - 1:
                direc[n] = new
                press[n] = so_far
            else:
                press[n] = so_far + new

    even = lax.rem(lane // 32, 2) == 0
    for row in range(4):
        packed = jnp.where(even, roll_lanes(press[row], -MARGIN), roll_lanes(press[row + 4], MARGIN))
        for quarter in range(QUARTERS):
            part_send[quarter, row] = packed[quarter * 8 : quarter * 8 + 8]

    def part_copy(slot, target):
        return pltpu.make_async_remote_copy(
            src_ref=part_send.at[target], dst_ref=part_recv.at[slot], send_sem=part_ss.at[target],
            recv_sem=part_rs.at[slot], device_id={"shift": target}, device_id_type=MESH,
        )

    for step in range(1, QUARTERS):
        part_copy(shift, lax.rem(shift + step, QUARTERS)).start()
    part_recv[shift] = part_send[shift]
    for step in range(1, QUARTERS):
        slot = lax.rem(shift + step, QUARTERS)
        part_copy(slot, slot).wait_recv()

    for row in range(4):
        parts = [part_recv[slot, row] for slot in range(QUARTERS)]
        first = (parts[0] + parts[1]) + (parts[2] + parts[3])
        second = (parts[0] * parts[0] + parts[1] * parts[1]) + (parts[2] * parts[2] + parts[3] * parts[3])
        mean = first * (1.0 / QUARTERS)
        var = (second - first * mean) * (1.0 / (QUARTERS - 1))
        brick_send[0, row] = jnp.where(left8, mean, roll_lanes(var, 64))
        brick_send[1, row] = jnp.where(left8, roll_lanes(mean, 64), var)

    def brick_copy(bx, step, slot):
        return pltpu.make_async_remote_copy(
            src_ref=brick_send.at[bx], dst_ref=brick_recv.at[slot],
            send_sem=brick_ss.at[bx * QUARTERS + step], recv_sem=brick_rs.at[slot],
            device_id={"shift": lax.rem(shift + step, QUARTERS), "space": bx * QUARTERS + shift},
            device_id_type=MESH,
        )

    for step in range(QUARTERS):
        for bx in range(2):
            if step:
                brick_copy(bx, step, me).start()
            else:

                @pl.when(me != bx * QUARTERS + shift)
                def _():
                    brick_copy(bx, step, me).start()

    @pl.when(own)
    def _():
        brick_recv[me] = brick_send[me // QUARTERS]

    for slab in range(SLABS):

        @pl.when(jnp.logical_not(jnp.logical_and(own, me == slab)))
        def _():
            brick_copy(0, 1, slab).wait_recv()

    group = lax.broadcasted_iota(jnp.int32, (8, 128), 1) // 32
    for which, out_ref in enumerate((mean_ref, var_ref)):
        for high in range(2):
            place_in = which * 2 + high
            for row in range(4):
                for side in range(2):
                    done = None
                    for lap in range(4):
                        piece = roll_lanes(brick_recv[side * 4 + lap, row], 32 * (lap - place_in))
                        done = piece if done is None else jnp.where(group == lap, piece, done)
                    out_ref[high * 4 + row, :, side * 128 : side * 128 + 128] = done

    for step in range(1, SLABS):
        target = lax.rem(me + step, SLABS)
        space_copy(src_send, src_recv, src_ss, src_rs, target, target).wait_send()
        space_copy(perm_send, perm_recv, perm_ss, perm_rs, target, target).wait_send()
    for step in range(1, QUARTERS):
        target = lax.rem(shift + step, QUARTERS)
        part_copy(target, target).wait_send()
    for step in range(QUARTERS):
        for bx in range(2):
            if step:
                brick_copy(bx, step, me).wait_send()
            else:

                @pl.when(me != bx * QUARTERS + shift)
                def _():
                    brick_copy(bx, step, me).wait_send()


def slab_shards(coefficients, source):
    modes_count = coefficients.shape[-1]
    cells_z = modes_count // 2
    angle = 2.0 * np.pi / modes_count * (np.outer(np.arange(modes_count), np.arange(cells_z)) % modes_count)
    exact = np.stack([np.cos(angle), np.sin(angle)])
    high = exact.astype(ml_dtypes.bfloat16)
    low = (exact - high.astype(np.float64)).astype(ml_dtypes.bfloat16)
    table = jnp.asarray(np.stack([high, low]))
    f32 = jnp.float32
    field = pltpu.VMEM((8, 32, 128), f32)
    vmem = pl.BlockSpec(memory_space=pltpu.VMEM)
    dma = pltpu.SemaphoreType.DMA
    out = jax.ShapeDtypeStruct((8, 8, cells_z), f32)
    mean, var = pl.pallas_call(
        slab_kernel,
        out_shape=(out, out),
        in_specs=[vmem, vmem, pl.BlockSpec(memory_space=pl.ANY)],
        out_specs=(vmem, vmem),
        scratch_shapes=[
            pltpu.VMEM(table.shape, jnp.bfloat16),
            pltpu.VMEM((8, 4, 8, 128), f32), pltpu.VMEM((8, 4, 8, 128), f32),
            field, field, field, field, field, field, field, field, field,
            pltpu.VMEM((4, 4, 8, 128), f32), pltpu.VMEM((4, 4, 8, 128), f32),
            pltpu.VMEM((2, 4, 8, 128), f32), pltpu.VMEM((8, 4, 8, 128), f32),
            dma, dma((8,)), dma((8,)), dma((8,)), dma((8,)), dma((4,)), dma((4,)), dma((8,)), dma((8,)),
        ],
        compiler_params=pltpu.CompilerParams(
            collective_id=0, has_side_effects=True, vmem_limit_bytes=32 * 1024 * 1024
        ),
    )(coefficients.reshape(2, 64, modes_count), source[0], table)
    return mean[None], var[None]


def solution(mesh):
    in_specs = (P("shift", None, None, "space", None, None), P("space", None, None, None))
    out_specs = (P("space", None, None, None), P("space", None, None, None))

    def chosen(coefficients, source):
        slabs = (
            coefficients.shape == (1, 2, 2, 1, 32, 512)
            and source.shape == (1, 8, 8, 256)
            and mesh.shape["space"] == SLABS
            and mesh.shape["shift"] == QUARTERS
        )
        return slab_shards(coefficients, source) if slabs else shards(coefficients, source)

    return jax.shard_map(chosen, mesh=mesh, in_specs=in_specs, out_specs=out_specs, check_vma=False)
```

```python
import functools
import math

import jax
import jax.numpy as jnp
import ml_dtypes
import numpy as np
from jax import lax
from jax.experimental import pallas as pl
from jax.experimental.pallas import tpu as pltpu
from jax.sharding import PartitionSpec as P

ITERS = 4
MESH = pl.DeviceIdType.MESH
SLABS = 8
SLAB = 32
MARGIN = 16
QUARTERS = 4


reaction = 0.02
low_bound = 0.05
high_bound = 2.0
centre = 0.5 * (low_bound + high_bound)
half_width = 0.5 * (high_bound - low_bound)
sigma_one = centre / half_width


def passed_along(value, axis, steps):
    count = lax.axis_size(axis)
    first, last = (max(0, -steps), min(count, count - steps))
    return lax.ppermute(value, axis, [(source, source + steps) for source in range(first, last)])


def harmonic(left, right):
    return 2.0 * left * right / (left + right)


def carry_first(layer, offset):
    return passed_along(layer, "space", offset)


def carry_second(layer, offset):
    return passed_along(layer, "space", offset)


def lower_and_upper(
    pressure_field, which_axis, index_step, axis_position, bricks_along, halo_holder
):
    extent = pressure_field.shape[which_axis]
    highest_layer = lax.slice_in_dim(pressure_field, extent - 1, extent, axis=which_axis)
    lowest_layer = lax.slice_in_dim(pressure_field, 0, 1, axis=which_axis)
    lower_mask = (axis_position > 0).astype(jnp.float32)
    upper_mask = (axis_position < bricks_along - 1).astype(jnp.float32)
    received_below = halo_holder(highest_layer, index_step) * lower_mask
    received_above = halo_holder(lowest_layer, -index_step) * upper_mask
    lower = jnp.concatenate(
        [received_below, lax.slice_in_dim(pressure_field, 0, extent - 1, axis=which_axis)],
        axis=which_axis,
    )
    upper = jnp.concatenate(
        [lax.slice_in_dim(pressure_field, 1, extent, axis=which_axis), received_above],
        axis=which_axis,
    )
    return (lower, upper)


def along_depth(pressure_field, which_axis):
    extent = pressure_field.shape[which_axis]
    blank = jnp.zeros_like(lax.slice_in_dim(pressure_field, 0, 1, axis=which_axis))
    lower = jnp.concatenate(
        [blank, lax.slice_in_dim(pressure_field, 0, extent - 1, axis=which_axis)], axis=which_axis
    )
    upper = jnp.concatenate(
        [lax.slice_in_dim(pressure_field, 1, extent, axis=which_axis), blank], axis=which_axis
    )
    return (lower, upper)


def operate(pressure_field, weight_list, finders):
    total = reaction * pressure_field
    for which_axis in range(3):
        lower, upper = finders[which_axis](pressure_field)
        weight_lower, weight_upper = weight_list[which_axis]
        total = (
            total
            + weight_upper * (pressure_field - upper)
            + weight_lower * (pressure_field - lower)
        )
    return total


def shards(coefficients, source):
    n_space = lax.axis_size("space")
    bricks_first = max(2, n_space // 8)
    bricks_second = n_space // bricks_first
    position = lax.axis_index("space")
    brick_x = position // bricks_second
    brick_y = position % bricks_second
    local = coefficients[0]
    modes_count = local.shape[-1]
    columns = local.shape[3]
    cells_z = modes_count // 2
    pencils = local.reshape(2, bricks_first * columns, modes_count)
    modes = lax.broadcasted_iota(jnp.int32, (modes_count, cells_z), 0)
    cells = lax.broadcasted_iota(jnp.int32, (modes_count, cells_z), 1)
    angle = (modes * cells % modes_count).astype(jnp.float32) * (2.0 * math.pi / modes_count)
    logperm = jnp.dot(
        pencils[0],
        jnp.cos(angle),
        precision=lax.Precision.HIGHEST,
        preferred_element_type=jnp.float32,
    )
    logperm = logperm + jnp.dot(
        pencils[1],
        jnp.sin(angle),
        precision=lax.Precision.HIGHEST,
        preferred_element_type=jnp.float32,
    )
    perm_rows = jnp.exp(logperm)
    brick_cols = columns // bricks_second
    n_shift = lax.axis_size("shift")
    outgoing = perm_rows.reshape(n_space, 1, brick_cols, cells_z)
    arrived = lax.all_to_all(outgoing, "space", split_axis=0, concat_axis=1, tiled=True)
    perm = arrived.reshape(n_space, brick_cols, cells_z)

    def find_first(pressure_field):
        return lower_and_upper(pressure_field, 0, bricks_second, brick_x, bricks_first, carry_first)

    def find_second(pressure_field):
        return lower_and_upper(pressure_field, 1, 1, brick_y, bricks_second, carry_second)

    def find_third(pressure_field):
        return along_depth(pressure_field, 2)

    residual = source[0]
    finders = [find_first, find_second, find_third]
    weight_list = []
    diagonal = reaction + jnp.zeros_like(perm)
    for which_axis in range(3):
        lower, upper = finders[which_axis](perm)
        weight_lower = harmonic(perm, lower)
        weight_upper = harmonic(perm, upper)
        weight_list.append((weight_lower, weight_upper))
        diagonal = diagonal + (weight_lower + weight_upper)
    pressure = jnp.zeros_like(perm)
    direction = residual / diagonal / centre
    ratio_now = 1.0 / sigma_one
    for sweep_index in range(ITERS):
        pressure = pressure + direction
        residual = residual - operate(direction, weight_list, finders)
        ratio_next = 1.0 / (2.0 * sigma_one - ratio_now)
        direction = ratio_next * ratio_now * direction + 2.0 * ratio_next / half_width * (
            residual / diagonal
        )
        ratio_now = ratio_next
    pressure = pressure + direction
    first, second = lax.psum((pressure, pressure * pressure), "shift")
    pressure_mean = first / n_shift
    pressure_variance = (second - first * pressure_mean) / (n_shift - 1)
    return (pressure_mean[None], pressure_variance[None])


def lanes_of(value):
    return lax.broadcasted_iota(jnp.int32, value.shape, value.ndim - 1)


def roll_lanes(value, shift):
    shift = shift % value.shape[-1]
    return pltpu.roll(value, shift, value.ndim - 1) if shift else value


def window(low, high, slab, offset):
    start = (SLAB * slab - MARGIN) % 128
    shift = 128 - start + offset
    begin = SLAB * slab - MARGIN
    if begin + 64 <= 128 or slab == 0:
        return roll_lanes(low, shift)
    if begin >= 128:
        return roll_lanes(high, shift)
    return jnp.where(
        lanes_of(low) < 128 - start + offset, roll_lanes(low, shift), roll_lanes(high, shift)
    )


def window_pair(first, second, slab):
    left = window(first[..., :128], first[..., 128:], slab, 0)
    right = window(second[..., :128], second[..., 128:], slab, 64)
    return jnp.where(lanes_of(left) < 64, left, right)


def slab_kernel(
    coef_hbm, source_hbm, table_hbm,
    moment_ref,
    coef_ref, source_ref, table, src_send, src_recv, perm_send, perm_recv, w_x, w_y, w_z, rdiag, resid, direc, press,
    part_send, part_recv,
    source_sem, coef_sem, table_sem, src_ss, src_rs, share_ss, share_rs, perm_ss, perm_rs,
    part_ss, part_rs, hand_ss, hand_rs,
):
    shift = lax.axis_index("shift")
    me = lax.axis_index("space")
    side_y, core = shift // 2, lax.rem(shift, 2)
    partner = 2 * side_y + (1 - core)
    across = 2 * (1 - side_y) + core

    source_copies = [
        pltpu.make_async_copy(source_hbm.at[shift + 4 * half], source_ref.at[half], source_sem.at[half])
        for half in range(2)
    ]
    coef_copy = pltpu.make_async_copy(coef_hbm, coef_ref, coef_sem)
    table_copy = pltpu.make_async_copy(table_hbm, table, table_sem)
    for copy in (*source_copies, coef_copy, table_copy):
        copy.start()

    barrier = pltpu.get_barrier_semaphore()

    def greet(to_shift, to_space):
        pl.semaphore_signal(
            barrier, inc=1, device_id={"shift": to_shift, "space": to_space}, device_id_type=MESH
        )

    for step in range(SLABS):
        other = lax.rem(me + step, SLABS)
        if step:
            greet(shift, other)
        greet(across, other)
    greet(partner, me)
    greet(2 * (1 - side_y) + (1 - core), me)

    for copy in source_copies:
        copy.wait()
    for slab in range(SLABS):
        src_send[slab] = window_pair(source_ref[0], source_ref[1], slab)

    pl.semaphore_wait(barrier, 2 * SLABS + 1)

    def space_copy(send, recv, ss, rs, slot, target):
        return pltpu.make_async_remote_copy(
            src_ref=send.at[target], dst_ref=recv.at[slot], send_sem=ss.at[target],
            recv_sem=rs.at[slot], device_id={"space": target}, device_id_type=MESH,
        )

    def source_copy(slot, target):
        return pltpu.make_async_remote_copy(
            src_ref=src_send.at[target], dst_ref=src_recv.at[shift, slot], send_sem=src_ss.at[target],
            recv_sem=src_rs.at[slot], device_id={"space": target}, device_id_type=MESH,
        )

    def share_copy(slot, target):
        return pltpu.make_async_remote_copy(
            src_ref=src_recv.at[slot], dst_ref=src_recv.at[slot], send_sem=share_ss.at[target],
            recv_sem=share_rs.at[slot], device_id={"shift": target}, device_id_type=MESH,
        )

    for step in range(1, SLABS):
        source_copy(me, lax.rem(me + step, SLABS)).start()
    src_recv[shift, me] = src_send[me]

    coef_copy.wait()
    real, imag = coef_ref[0], coef_ref[1]
    real_hi, imag_hi = real.astype(jnp.bfloat16), imag.astype(jnp.bfloat16)
    real_lo = (real - real_hi.astype(jnp.float32)).astype(jnp.bfloat16)
    imag_lo = (imag - imag_hi.astype(jnp.float32)).astype(jnp.bfloat16)
    table_copy.wait()
    dot = functools.partial(jnp.dot, preferred_element_type=jnp.float32)
    rows = real.shape[0]
    both = dot(jnp.concatenate([real_hi, real_lo], 0), table[0, 0])
    both = both + dot(jnp.concatenate([imag_hi, imag_lo], 0), table[0, 1])
    rest = dot(real_hi, table[1, 0]) + dot(imag_hi, table[1, 1])
    perm = jnp.exp(both[:rows] + (both[rows:] + rest))
    half = rows // 2
    for slab in range(SLABS):
        perm_send[slab] = window_pair(perm[:half], perm[half:], slab)
    for step in range(1, SLABS):
        space_copy(perm_send, perm_recv, perm_ss, perm_rs, me, lax.rem(me + step, SLABS)).start()
    perm_recv[me] = perm_send[me]

    for step in range(1, SLABS):
        slot = lax.rem(me + step, SLABS)
        source_copy(slot, slot).wait_recv()
    for step in range(1, QUARTERS):
        share_copy(shift, lax.rem(shift + step, QUARTERS)).start()

    for step in range(1, SLABS):
        slot = lax.rem(me + step, SLABS)
        space_copy(perm_send, perm_recv, perm_ss, perm_rs, slot, slot).wait_recv()

    shape = (32, 128)
    lane = lax.broadcasted_iota(jnp.int32, shape, 1)
    sub = lax.broadcasted_iota(jnp.int32, shape, 0)
    place = SLAB * me - MARGIN + lax.rem(lane, 64)
    inner_z = jnp.logical_and(place != -1, place != 255)
    inner_y = sub != 31
    inner_x = lane < 64

    def next_y(value):
        return pltpu.roll(value, 31, 0)

    def last_y(value):
        return pltpu.roll(value, 1, 0)

    def next_z(value):
        return roll_lanes(value, 127)

    def last_z(value):
        return roll_lanes(value, 1)

    def face_x(n):
        upper = roll_lanes(perm_recv[0], 64) if n == 7 else perm_recv[n + 1]
        weight = harmonic(perm_recv[n], upper)
        return jnp.where(inner_x, weight, 0.0) if n == 7 else weight

    last = face_x(7)
    w_x[7] = last
    lower_x = roll_lanes(last, 64)
    for n in range(8):
        cell = perm_recv[n]
        if n < 7:
            last = face_x(n)
            w_x[n] = last
        else:
            last = w_x[7]
        up_y = jnp.where(inner_y, harmonic(cell, next_y(cell)), 0.0)
        up_z = jnp.where(inner_z, harmonic(cell, next_z(cell)), 0.0)
        w_y[n] = up_y
        w_z[n] = up_z
        diagonal = reaction + (lower_x + last) + (last_y(up_y) + up_y) + (last_z(up_z) + up_z)
        rdiag[n] = 1.0 / diagonal
        lower_x = last

    for step in range(1, QUARTERS):
        slot = lax.rem(shift + step, QUARTERS)
        share_copy(slot, slot).wait_recv()
    left8 = lax.broadcasted_iota(jnp.int32, (8, 128), 1) < 64
    for n in range(8):
        for brick_y in range(QUARTERS):
            near, far = src_recv[n % 4, brick_y], src_recv[n % 4, QUARTERS + brick_y]
            if n < 4:
                far = roll_lanes(far, 64)
            else:
                near = roll_lanes(near, 64)
            piece = jnp.where(left8, near, far)
            rows_y = slice(brick_y * 8, brick_y * 8 + 8)
            resid[n, rows_y] = piece
            direc[n, rows_y] = piece * rdiag[n, rows_y] * (1.0 / centre)

    ratio_now = 1.0 / sigma_one
    for sweep in range(ITERS):
        ratio_next = 1.0 / (2.0 * sigma_one - ratio_now)
        keep, gain = ratio_next * ratio_now, 2.0 * ratio_next / half_width
        ratio_now = ratio_next
        first_next = roll_lanes(direc[0], 64)
        flux_last = w_x[7] * (direc[7] - first_next)
        lower_flux = roll_lanes(flux_last, 64)
        for n in range(8):
            now = direc[n]
            flux = w_x[n] * (now - direc[n + 1]) if n < 7 else flux_last
            flux_y = w_y[n] * (now - next_y(now))
            flux_z = w_z[n] * (now - next_z(now))
            total = reaction * now + (flux - lower_flux)
            total = total + (flux_y - last_y(flux_y)) + (flux_z - last_z(flux_z))
            lower_flux = flux
            left_over = resid[n] - total
            if sweep < ITERS - 1:
                resid[n] = left_over
            new = keep * now + gain * (left_over * rdiag[n])
            so_far = now + press[n] if sweep else now
            if sweep < ITERS - 1:
                direc[n] = new
                press[n] = so_far
            else:
                press[n] = so_far + new

    group = lane // 32
    for bx in range(2):
        for tile in range(2):
            packed = None
            for quad in range(4):
                piece = roll_lanes(press[quad * 2 + tile], 32 * quad - 64 * bx - MARGIN)
                packed = piece if packed is None else jnp.where(group == quad, piece, packed)
            for brick_y in range(QUARTERS):
                part_send[bx * QUARTERS + brick_y, tile] = packed[brick_y * 8 : brick_y * 8 + 8]

    def part_copy(from_shift, from_slab, to_side, to_shift, target):
        return pltpu.make_async_remote_copy(
            src_ref=part_send.at[target], dst_ref=part_recv.at[from_shift, from_slab],
            send_sem=part_ss.at[to_side, target], recv_sem=part_rs.at[from_shift, from_slab],
            device_id={"shift": to_shift, "space": target}, device_id_type=MESH,
        )

    def hand_copy(of_shift, half):
        part = part_recv.at[of_shift, pl.ds(4 * half, 4)]
        return pltpu.make_async_remote_copy(
            src_ref=part, dst_ref=part, send_sem=hand_ss.at[of_shift, half],
            recv_sem=hand_rs.at[of_shift, half], device_id={"shift": partner}, device_id_type=MESH,
        )

    for step in range(SLABS):
        target = lax.rem(me + step, SLABS)
        if step:
            part_copy(shift, me, 0, shift, target).start()
        part_copy(shift, me, 1, across, target).start()
    part_recv[shift, me] = part_send[me]

    for of_shift in (shift, across):
        for half in range(2):
            for slab in range(half * 4, half * 4 + 4):
                if of_shift is shift:

                    @pl.when(me != slab)
                    def _():
                        part_copy(shift, slab, 0, shift, slab).wait_recv()
                else:
                    part_copy(across, slab, 1, across, slab).wait_recv()
            hand_copy(of_shift, half).start()
    for of_side in range(2):
        for half in range(2):
            hand_copy(2 * of_side + (1 - core), half).wait_recv()

    group = lax.broadcasted_iota(jnp.int32, (8, 128), 1) // 32
    for tile in range(2):
        for side in range(2):
            sums = [[], []]
            for lap in range(4):
                parts = [part_recv[slot, side * 4 + lap, tile] for slot in range(QUARTERS)]
                sums[0].append((parts[0] + parts[1]) + (parts[2] + parts[3]))
                squares = [part * part for part in parts]
                sums[1].append((squares[0] + squares[1]) + (squares[2] + squares[3]))
            for which in range(2):
                for quad in range(4):
                    done = None
                    for lap in range(4):
                        piece = roll_lanes(sums[which][lap], 32 * (lap - quad))
                        done = piece if done is None else jnp.where(group == lap, piece, done)
                    moment_ref[which, quad * 2 + tile, :, side * 128 : side * 128 + 128] = done

    for step in range(SLABS):
        target = lax.rem(me + step, SLABS)
        if step:
            source_copy(target, target).wait_send()
            space_copy(perm_send, perm_recv, perm_ss, perm_rs, target, target).wait_send()
            part_copy(shift, me, 0, shift, target).wait_send()
        part_copy(shift, me, 1, across, target).wait_send()
    for step in range(1, QUARTERS):
        share_copy(shift, lax.rem(shift + step, QUARTERS)).wait_send()
    for of_shift in (shift, across):
        for half in range(2):
            hand_copy(of_shift, half).wait_send()


def slab_shards(coefficients, source):
    modes_count = coefficients.shape[-1]
    cells_z = modes_count // 2
    angle = 2.0 * np.pi / modes_count * (np.outer(np.arange(modes_count), np.arange(cells_z)) % modes_count)
    exact = np.stack([np.cos(angle), np.sin(angle)])
    high = exact.astype(ml_dtypes.bfloat16)
    low = (exact - high.astype(np.float64)).astype(ml_dtypes.bfloat16)
    table = jnp.asarray(np.stack([high, low]))
    f32 = jnp.float32
    field = pltpu.VMEM((8, 32, 128), f32)
    dma = pltpu.SemaphoreType.DMA
    anywhere = pl.BlockSpec(memory_space=pl.ANY)
    moments = pl.pallas_call(
        slab_kernel,
        out_shape=jax.ShapeDtypeStruct((2, 8, 8, cells_z), f32),
        in_specs=[anywhere, anywhere, anywhere],
        out_specs=pl.BlockSpec(memory_space=pltpu.VMEM),
        scratch_shapes=[
            pltpu.VMEM((2, 64, modes_count), f32), pltpu.VMEM((2, 8, cells_z), f32),
            pltpu.VMEM(table.shape, jnp.bfloat16),
            pltpu.VMEM((8, 8, 128), f32), pltpu.VMEM((4, 8, 8, 128), f32),
            field, field, field, field, field, field, field, field, field,
            pltpu.VMEM((8, 2, 8, 128), f32), pltpu.VMEM((4, 8, 2, 8, 128), f32),
            dma((2,)), dma, dma, dma((8,)), dma((8,)), dma((4,)), dma((4,)), dma((8,)), dma((8,)),
            dma((2, 8)), dma((4, 8)), dma((4, 2)), dma((4, 2)),
        ],
        compiler_params=pltpu.CompilerParams(
            collective_id=0, has_side_effects=True, vmem_limit_bytes=56 * 1024 * 1024
        ),
    )(coefficients.reshape(2, 64, modes_count), source[0], table)
    first, second = moments[0], moments[1]
    mean = first / QUARTERS
    var = (second - first * mean) / (QUARTERS - 1)
    return mean[None], var[None]


def solution(mesh):
    in_specs = (P("shift", None, None, "space", None, None), P("space", None, None, None))
    out_specs = (P("space", None, None, None), P("space", None, None, None))

    def chosen(coefficients, source):
        slabs = (
            coefficients.shape == (1, 2, 2, 1, 32, 512)
            and source.shape == (1, 8, 8, 256)
            and mesh.shape["space"] == SLABS
            and mesh.shape["shift"] == QUARTERS
        )
        return slab_shards(coefficients, source) if slabs else shards(coefficients, source)

    return jax.shard_map(chosen, mesh=mesh, in_specs=in_specs, out_specs=out_specs, check_vma=False)
```
